128 devices in a mesh: freq: 4 (over x), blk: 32 (over z, y, core).
Axes of the slice: x: 4, y: 4, z: 4, core: 2. Of those that a mesh axis runs over, the one named last changes fastest.
Arguments:
- series: bfloat16 [32, 128, 6000], P('blk', 'freq'), may hold values from -24 to 24
- tapers: float32 [5, 6000], replicated, may hold values from -0.078125 to 0.078125
- live_channels: int32 [32], P('blk'), may hold values from 64 to 128, as said below
- pair_offset: int32 [32, 5], P('blk'), may hold values from 0 to 4, as said below
- pair_count: int32 [32], P('blk'), may hold values from 1 to 5, as said below
Outputs:
- csdm: float32 [32, 5, 2, 16, 128, 128], P('blk', None, None, 'freq')
The draws below stay inside these ranges and needn't reach their ends.
Inputs may be any that keep to these rules, and one draw needn't show every extreme that they name: `live_channels`: one block in every draw has all 128 channels working. `pair_offset`: the first pair_count[i] entries of row i are distinct offsets in ascending order, the used ones; the rest of the row holds the remaining offsets of 0 to 4 in ascending order. `pair_count`: some block in every draw uses all 5 slots.
All inputs are finite; a program needn't handle non-finite values.
Results may differ from the reference program's by a relative error of at most 0.0043.
Values may be sent and summed in bfloat16 or wider, within the bound.
No kernel may reach another device: no remote copies, remote signals or barrier semaphores. Data moves between devices by JAX's collectives and lax.ppermute only.
A program may use at most 128 MiB of HBM per device.

```python
import math
import jax
import jax.numpy as jnp
from jax import lax

TSAMP = 6000
NF = 2048
K = 5
BS = 128
BW = 128
SLOTS = 5
NBLOCKS = 32
NBANDS = 16
NFFT = 4096


def pair_helper(key):
    count = jax.random.randint(jax.random.fold_in(key, 11), (NBLOCKS,), 1, SLOTS + 1)
    chosen = jax.random.randint(jax.random.fold_in(key, 12), (), 0, NBLOCKS)
    count = jnp.where(jnp.arange(NBLOCKS) == chosen, SLOTS, count).astype(jnp.int32)
    scores = jax.random.randint(jax.random.fold_in(key, 13), (NBLOCKS, SLOTS), 0, 1000)
    scores = scores * SLOTS + jnp.arange(SLOTS)[None, :]
    ranking = jnp.argsort(jnp.argsort(scores, axis=1), axis=1)
    used = ranking < count[:, None]
    sort_keys = jnp.where(used, 0, SLOTS) + jnp.arange(SLOTS)[None, :]
    offsets = jnp.sort(sort_keys, axis=1) % SLOTS
    return (count, offsets.astype(jnp.int32))


def draw_pair_offset(key, part):
    count, offsets = pair_helper(key)
    return offsets


def draw_pair_count(key, part):
    count, offsets = pair_helper(key)
    return count


def draw_live_channels(key, part):
    key = jax.random.fold_in(key, 3)
    counts = jax.random.randint(key, (NBLOCKS,), BS // 2, BS + 1)
    chosen = jax.random.randint(jax.random.fold_in(key, 4), (), 0, NBLOCKS)
    return jnp.where(jnp.arange(NBLOCKS) == chosen, BS, counts).astype(jnp.int32)


def level_of(stream_key, dims, split, smallest, high):
    factor_of, own = 1.0, jax.random.fold_in(stream_key, 6)
    for dim, blocks in split:
        draws = jnp.exp(jax.random.uniform(jax.random.fold_in(own, dim), (blocks,), jnp.float32, smallest / len(split), high / len(split)))
        factor_of = factor_of * jnp.repeat(draws, dims[dim] // blocks).reshape([-1 if axis == dim else 1 for axis in range(len(dims))])
    return factor_of


def centred(key, extent, deviation, reach, split=(), kind=jnp.bfloat16):
    level = level_of(key, extent, split, -0.22, 0.18) if split else 1.0
    array = jax.random.normal(key, extent, jnp.float32) * deviation * level
    return jnp.minimum(jnp.maximum(array, -reach), reach).astype(kind)


def setup_inputs(seed: int = 0) -> dict:
    splits = jax.random.split(jax.random.key(seed), 6)
    series = centred(splits[0], (NBLOCKS, BS, TSAMP), 4.0, 24.0, ((0, 32), (1, 4)))
    tapers = centred(splits[1], (K, TSAMP), TSAMP ** -0.5, 0.078125, (), jnp.float32)
    live_channels = draw_live_channels(jax.random.fold_in(splits[5], 71), 0)
    pair_offset = draw_pair_offset(jax.random.fold_in(splits[5], 71), 0)
    pair_count = draw_pair_count(jax.random.fold_in(splits[5], 71), 0)
    return {"series": series, "tapers": tapers, "live_channels": live_channels, "pair_offset": pair_offset, "pair_count": pair_count}


def dft_table(first_bin, count, length, period):
    samples = jnp.arange(length).astype(jnp.int32)
    bins = (first_bin + jnp.arange(count)).astype(jnp.int32)
    phase = (samples[:, None] * bins[None, :]) % period
    angle = phase.astype(jnp.float32) * (2.0 * math.pi / period)
    return jnp.concatenate([jnp.cos(angle), -jnp.sin(angle)], axis=1).astype(jnp.bfloat16)


def cross_band(mine, other):
    rotated = jnp.stack([-other[:, :, 1], other[:, :, 0]], axis=2)
    mine_f = mine.astype(jnp.float32)
    real_part = jnp.einsum("kcpbw,kdpbw->bcd", mine_f, other.astype(jnp.float32))
    imag_part = jnp.einsum("kcpbw,kdpbw->bcd", mine_f, rotated.astype(jnp.float32))
    return jnp.stack([real_part, imag_part]) * (1.0 / (K * BW))


def reference(series, tapers, live_channels, pair_offset, pair_count):
    table = dft_table(0, NF, TSAMP, NFFT)

    def block_spectra(index):
        channel = jnp.arange(BS).astype(jnp.int32)
        weight_mask = (channel < live_channels[index]).astype(jnp.float32)
        tapered = (series[index].astype(jnp.float32)[None] * tapers[:, None, :] * weight_mask[None, :, None]).astype(jnp.bfloat16)
        product = jnp.dot(tapered.reshape(K * BS, TSAMP), table, preferred_element_type=jnp.float32)
        return product.reshape(K, BS, 2, NF).astype(jnp.bfloat16)

    block_ids = jnp.arange(NBLOCKS).astype(jnp.int32)
    spectra = lax.map(block_spectra, block_ids)

    def block_pairs(index):
        mine = spectra[index].reshape(K, BS, 2, NBANDS, BW)
        results = []
        for position in range(SLOTS):
            partner_index = ((index + pair_offset[index, position]) % NBLOCKS).astype(jnp.int32)
            other = spectra[partner_index].reshape(K, BS, 2, NBANDS, BW)
            live_slot = (position < pair_count[index]).astype(jnp.float32)
            results.append(cross_band(mine, other) * live_slot)
        return jnp.stack(results)

    return lax.map(block_pairs, block_ids)
```

```python
import functools

import jax
import jax.numpy as jnp
import ml_dtypes
import numpy as np
from jax import lax
from jax.experimental import pallas as pl
from jax.experimental.pallas import tpu as pltpu
from jax.sharding import Mesh
from jax.sharding import PartitionSpec as P

NF = 2048
K = 5
BW = 128
PERIOD = 2 * NF
HALF = PERIOD // 2
SLOTS = 5
RING = 4
OWNERS = RING * RING
VMEM_LIMIT = 56 * 1024 * 1024


def half_period_tables():
    samples = np.arange(HALF, dtype=np.int64)
    bins = np.stack(
        [
            np.concatenate(
                [(RING * (owner % RING) + owner // RING) * BW + 2 * np.arange(BW // 2) + parity
                 for owner in range(OWNERS)]
            )
            for parity in range(2)
        ]
    )
    angle = ((samples[None, :, None] * bins[:, None, :]) % PERIOD) * (2.0 * np.pi / PERIOD)
    parts = np.stack([np.cos(angle), -np.sin(angle)], axis=2)
    parts = parts.reshape(2, HALF, 2, OWNERS, BW // 2).transpose(3, 0, 1, 2, 4)
    parts = parts.reshape(OWNERS // 2, 2, 2, HALF, BW).transpose(0, 2, 3, 1, 4)
    return parts.reshape(OWNERS // 2, 2, HALF, 2 * BW).astype(ml_dtypes.bfloat16)


def spectra_kernel(scalars, series, tapers, table, out, even, odd):
    rows, samples = series.shape

    @pl.when(pl.program_id(0) == 0)
    def _():
        live, first = scalars[0], scalars[1]
        channel = first + lax.broadcasted_iota(jnp.int32, (rows, HALF), 0)
        working = channel < live

        def tapered(k, begin, end):
            product = series[:, begin:end].astype(jnp.float32) * tapers[k : k + 1, begin:end]
            if end - begin < HALF:
                product = jnp.concatenate(
                    [product, jnp.zeros((rows, HALF - (end - begin)), jnp.float32)], axis=1
                )
            product = jnp.where(working, product, 0.0)
            return product.astype(jnp.bfloat16).astype(jnp.float32)

        for k in range(K):
            ends = tapered(k, 0, HALF) + tapered(k, 2 * HALF, samples)
            middle = tapered(k, HALF, 2 * HALF)
            even[k * rows : (k + 1) * rows, :] = (ends + middle).astype(jnp.bfloat16)
            odd[k * rows : (k + 1) * rows, :] = (ends - middle).astype(jnp.bfloat16)

    for parity, folded in enumerate((even, odd)):
        bins = jnp.dot(folded[...], table[0, parity], preferred_element_type=jnp.float32)
        bins = bins.astype(jnp.bfloat16)
        out[0, :, parity * BW : (parity + 1) * BW] = bins[:, :BW]
        out[1, :, parity * BW : (parity + 1) * BW] = bins[:, BW:]


def block_spectra(scalars, series, tapers, table):
    rows, samples = series.shape
    return pl.pallas_call(
        spectra_kernel,
        grid=(OWNERS // 2,),
        in_specs=[
            pl.BlockSpec(memory_space=pltpu.SMEM),
            pl.BlockSpec((rows, samples), lambda step: (0, 0)),
            pl.BlockSpec((K, samples), lambda step: (0, 0)),
            pl.BlockSpec((1, 2, HALF, 2 * BW), lambda step: (step, 0, 0, 0)),
        ],
        out_specs=pl.BlockSpec((2, K * rows, 2 * BW), lambda step: (step, 0, 0)),
        out_shape=jax.ShapeDtypeStruct((OWNERS, K * rows, 2 * BW), jnp.bfloat16),
        scratch_shapes=[
            pltpu.VMEM((K * rows, HALF), jnp.bfloat16),
            pltpu.VMEM((K * rows, HALF), jnp.bfloat16),
        ],
        compiler_params=pltpu.CompilerParams(vmem_limit_bytes=VMEM_LIMIT),
        cost_estimate=pl.CostEstimate(
            flops=2 * K * rows * HALF * 2 * NF, bytes_accessed=20_000_000, transcendentals=0
        ),
    )(scalars, series, tapers, table)


def pair_kernel(targets, held, scalars, *refs):
    outs = refs[-RING:]
    mine_refs, other_refs = refs[: (len(refs) - RING) // 2], refs[(len(refs) - RING) // 2 : -RING]
    y, core = scalars[0], scalars[1]
    rows = mine_refs[0].shape[1] // K

    def channels(group, at, k):
        source = group[0] if at < held else group[1]
        at = at if at < held else at - held
        piece = source[RING * at : RING * (at + 1), k * rows : (k + 1) * rows, :]
        return piece.reshape(RING * rows, 2 * BW)

    def rotated(spectrum):
        wide = spectrum.astype(jnp.float32)
        half = BW // 2
        parts = []
        for parity in range(2):
            at = parity * BW
            parts += [wide[:, at + half : at + BW], -wide[:, at : at + half]]
        return jnp.concatenate(parts, axis=1).astype(jnp.bfloat16)

    for target in targets:
        total = None
        for k in range(K):
            mine = channels(mine_refs, target, k)
            left = jnp.concatenate([mine, rotated(mine)], axis=0)
            later = [channels(other_refs, target + step, k) for step in range(3)]
            right = jnp.concatenate(
                [
                    channels(mine_refs, target, k),
                    jnp.where(core == 0, later[0], later[1]),
                    channels(mine_refs, target + 1, k),
                    jnp.where(core == 0, later[1], later[2]),
                    channels(mine_refs, target + 2, k),
                ],
                axis=0,
            )
            term = lax.dot_general(
                left, right, (((1,), (1,)), ((), ())), preferred_element_type=jnp.float32
            )
            total = term if total is None else total + term
        total = (total * (1.0 / (K * BW))).astype(jnp.bfloat16)
        distance = lax.rem(target - y + RING, RING)
        for step in range(RING):

            @pl.when(distance == step)
            def _():
                for offset in range(SLOTS):
                    piece = total[:, offset * BW : (offset + 1) * BW]
                    outs[step][offset, 0] = piece[:BW]
                    outs[step][offset, 1] = piece[BW:]


def pair_products(targets, scalars, mine, other):
    held = mine[0].shape[0] // RING
    whole = pl.BlockSpec(memory_space=pltpu.VMEM)
    return pl.pallas_call(
        functools.partial(pair_kernel, targets, held),
        in_specs=[pl.BlockSpec(memory_space=pltpu.SMEM)] + [whole] * (len(mine) + len(other)),
        out_specs=[whole] * RING,
        out_shape=[jax.ShapeDtypeStruct((SLOTS, 2, BW, BW), jnp.bfloat16)] * RING,
        compiler_params=pltpu.CompilerParams(vmem_limit_bytes=VMEM_LIMIT),
        cost_estimate=pl.CostEstimate(
            flops=2 * len(targets) * K * 2 * BW * 2 * BW * SLOTS * BW,
            bytes_accessed=4_000_000,
            transcendentals=0,
        ),
    )(scalars, *mine, *other)


def slots_kernel(scalars, *refs):
    out = refs[-1]
    early, late = refs[:RING], refs[RING : 2 * RING]
    y, count = scalars[0], scalars[1]

    def place(group):
        for distance in range(RING):
            band = lax.rem(y - distance + RING, RING)
            for slot in range(SLOTS):
                live = (slot < count).astype(jnp.float32)
                piece = group[distance][scalars[2 + slot]]
                out[slot, :, band] = piece.astype(jnp.float32) * live

    pl.when(y < RING // 2)(lambda: place(early))
    pl.when(y >= RING // 2)(lambda: place(late))


def slots_output(scalars, early, late):
    whole = pl.BlockSpec(memory_space=pltpu.VMEM)
    return pl.pallas_call(
        slots_kernel,
        in_specs=[pl.BlockSpec(memory_space=pltpu.SMEM)] + [whole] * (2 * RING),
        out_specs=whole,
        out_shape=jax.ShapeDtypeStruct((SLOTS, 2, RING, BW, BW), jnp.float32),
        compiler_params=pltpu.CompilerParams(vmem_limit_bytes=VMEM_LIMIT),
    )(scalars, *early, *late)


def sent_to(targets, pieces):
    moved = [pieces[0]]
    for distance in range(1, RING):
        routes = [((target - distance) % RING, target) for target in targets]
        moved.append(lax.ppermute(pieces[distance], "y", routes))
    return moved


def body(table, series, tapers, live_channels, pair_offset, pair_count):
    x, y, core = lax.axis_index("freq"), lax.axis_index("y"), lax.axis_index("core")
    rows = series.shape[1]
    first = jnp.stack([live_channels[0], x * rows]).astype(jnp.int32)
    spectra = block_spectra(first, series[0], tapers, table)
    mine = lax.all_to_all(spectra, ("y", "freq"), 0, 0)
    swap = [(0, 1), (1, 0)]
    next_plane = [(i, (i - 1) % RING) for i in range(RING)]
    ahead = lax.ppermute(mine[: OWNERS // 2], "z", next_plane)
    other = lax.ppermute(mine, "core", swap)
    place = jnp.stack([y, core]).astype(jnp.int32)
    early = pair_products((0, 1), place, [mine], [other])
    early = sent_to((0, 1), early)
    other_ahead = lax.ppermute(ahead, "core", swap)
    late = pair_products((2, 3), place, [mine, ahead], [other, other_ahead])
    late = sent_to((2, 3), late)
    last = jnp.concatenate([jnp.stack([y, pair_count[0]]), pair_offset[0]]).astype(jnp.int32)
    return slots_output(last, early, late)[None]


def solution(mesh):
    table = half_period_tables()
    grid = Mesh(
        mesh.devices.reshape(RING, RING, RING, 2), ("freq", "z", "y", "core")
    )
    blk = ("z", "y", "core")
    return jax.shard_map(
        functools.partial(body, table),
        mesh=grid,
        in_specs=(P(blk, "freq", None), P(), P(blk), P(blk, None), P(blk)),
        out_specs=P(blk, None, None, "freq", None, None),
        check_vma=False,
    )
```

```python
import functools

import jax
import jax.numpy as jnp
import ml_dtypes
import numpy as np
from jax import lax
from jax.experimental import pallas as pl
from jax.experimental.pallas import tpu as pltpu
from jax.sharding import Mesh
from jax.sharding import PartitionSpec as P

NF = 2048
K = 5
BW = 128
PERIOD = 2 * NF
HALF = PERIOD // 2
SLOTS = 5
RING = 4
OWNERS = RING * RING
VMEM_LIMIT = 24 * 1024 * 1024
STREAM_VMEM_LIMIT = 56 * 1024 * 1024


def half_period_tables():
    samples = np.arange(HALF, dtype=np.int64)
    bins = np.stack(
        [
            np.concatenate(
                [(RING * (owner % RING) + owner // RING) * BW + 2 * np.arange(BW // 2) + parity
                 for owner in range(OWNERS)]
            )
            for parity in range(2)
        ]
    )
    angle = ((samples[None, :, None] * bins[:, None, :]) % PERIOD) * (2.0 * np.pi / PERIOD)
    parts = np.stack([np.cos(angle), -np.sin(angle)], axis=2)
    parts = parts.reshape(2, HALF, 2, OWNERS, BW // 2).transpose(3, 0, 1, 2, 4)
    parts = parts.reshape(OWNERS // 2, 2, 2, HALF, BW).transpose(0, 2, 3, 1, 4)
    return parts.reshape(OWNERS // 2, 2, HALF, 2 * BW).astype(ml_dtypes.bfloat16)


def spectra_kernel(live_counts, series, tapers, table, out, even, odd):
    rows, samples = series.shape

    @pl.when(pl.program_id(0) == 0)
    def _():
        live, first = live_counts[0], lax.axis_index("freq") * rows
        channel = first + lax.broadcasted_iota(jnp.int32, (rows, HALF), 0)
        working = channel < live

        def tapered(k, begin, end):
            product = series[:, begin:end].astype(jnp.float32) * tapers[k : k + 1, begin:end]
            if end - begin < HALF:
                product = jnp.concatenate(
                    [product, jnp.zeros((rows, HALF - (end - begin)), jnp.float32)], axis=1
                )
            product = jnp.where(working, product, 0.0)
            return product.astype(jnp.bfloat16).astype(jnp.float32)

        for k in range(K):
            ends = tapered(k, 0, HALF) + tapered(k, 2 * HALF, samples)
            middle = tapered(k, HALF, 2 * HALF)
            even[k * rows : (k + 1) * rows, :] = (ends + middle).astype(jnp.bfloat16)
            odd[k * rows : (k + 1) * rows, :] = (ends - middle).astype(jnp.bfloat16)

    for parity, folded in enumerate((even, odd)):
        bins = jnp.dot(folded[...], table[0, parity], preferred_element_type=jnp.float32)
        bins = bins.astype(jnp.bfloat16)
        out[0, :, parity * BW : (parity + 1) * BW] = bins[:, :BW]
        out[1, :, parity * BW : (parity + 1) * BW] = bins[:, BW:]


def block_spectra(live_counts, series, tapers, table):
    rows, samples = series.shape
    return pl.pallas_call(
        spectra_kernel,
        grid=(OWNERS // 2,),
        in_specs=[
            pl.BlockSpec(memory_space=pltpu.SMEM),
            pl.BlockSpec((rows, samples), lambda step: (0, 0)),
            pl.BlockSpec((K, samples), lambda step: (0, 0)),
            pl.BlockSpec((1, 2, HALF, 2 * BW), lambda step: (step, 0, 0, 0)),
        ],
        out_specs=pl.BlockSpec((2, K * rows, 2 * BW), lambda step: (step, 0, 0)),
        out_shape=jax.ShapeDtypeStruct((OWNERS, K * rows, 2 * BW), jnp.bfloat16),
        scratch_shapes=[
            pltpu.VMEM((K * rows, HALF), jnp.bfloat16),
            pltpu.VMEM((K * rows, HALF), jnp.bfloat16),
        ],
        compiler_params=pltpu.CompilerParams(vmem_limit_bytes=STREAM_VMEM_LIMIT),
        cost_estimate=pl.CostEstimate(
            flops=2 * K * rows * HALF * 2 * NF, bytes_accessed=20_000_000, transcendentals=0
        ),
    )(live_counts, series, tapers, table)


def pair_kernel(wanted, *refs):
    later, mine_wide, other_wide = refs[-3:]
    outs = refs[-3 - RING : -3]
    inputs = refs[: -3 - RING]
    y, core = lax.axis_index("y"), lax.axis_index("core")
    rows = inputs[0].shape[1] // K
    half = BW // 2
    first = min(wanted)

    def channels(group, at, k):
        for source in group:
            if at < source.shape[0] // RING:
                piece = source[RING * at : RING * (at + 1), k * rows : (k + 1) * rows, :]
                return piece.reshape(RING * rows, 2 * BW)
            at -= source.shape[0] // RING

    def widened(group, wide, blocks):
        for block in blocks:
            to = (block - first) * BW
            for k in range(K):
                wide[to : to + BW, k * 2 * BW : (k + 1) * 2 * BW] = channels(group, block, k)

    same_of, crossed_of = {}, {}
    for target, offsets in wanted.items():
        same_of[target] = [target + offset // 2 for offset in offsets if offset % 2 == 0]
        crossed_of[target] = [target + offset // 2 for offset in offsets if offset % 2 == 1]
    same_blocks = set(wanted).union(*same_of.values())
    crossed_blocks = set().union(*crossed_of.values())
    widened(inputs[: len(inputs) // 2], mine_wide, sorted(same_blocks))
    widened(
        inputs[len(inputs) // 2 :],
        other_wide,
        sorted(crossed_blocks | {block + 1 for block in crossed_blocks}),
    )

    contract = (((1,), (1,)), ((), ()))
    for target, offsets in wanted.items():
        to = (target - first) * BW
        later[:BW, :] = mine_wide[to : to + BW, :]
        for part in range(2 * K):
            at = part * BW
            wide = mine_wide[to : to + BW, at : at + BW].astype(jnp.float32)
            turned = jnp.concatenate([wide[:, half:], -wide[:, :half]], axis=1)
            later[BW:, at : at + BW] = turned.astype(jnp.bfloat16)
        same, crossed = same_of[target], crossed_of[target]
        at = (same[0] - first) * BW
        partners = mine_wide[at : at + len(same) * BW, :]
        even = lax.dot_general(later[...], partners, contract, preferred_element_type=jnp.float32)
        even = (even * (1.0 / (K * BW))).astype(jnp.bfloat16)
        if crossed:
            at = pl.multiple_of((crossed[0] - first + core) * BW, BW)
            partners = other_wide[pl.ds(at, len(crossed) * BW), :]
            odd = lax.dot_general(
                later[...], partners, contract, preferred_element_type=jnp.float32
            )
            odd = (odd * (1.0 / (K * BW))).astype(jnp.bfloat16)
        distance = lax.rem(target - y + RING, RING)
        for step in range(RING):

            @pl.when(distance == step)
            def _():
                for at, offset in enumerate(offsets):
                    group, kind = (even, same) if offset % 2 == 0 else (odd, crossed)
                    column = kind.index(target + offset // 2) * BW
                    piece = group[:, column : column + BW]
                    outs[step][at, 0] = piece[:BW]
                    outs[step][at, 1] = piece[BW:]


def pair_products(wanted, mine, other):
    pairs = max(len(offsets) for offsets in wanted.values())
    reach = sum(block.shape[0] // RING for block in mine) - min(wanted)
    whole = pl.BlockSpec(memory_space=pltpu.VMEM)
    return pl.pallas_call(
        functools.partial(pair_kernel, wanted),
        in_specs=[whole] * (len(mine) + len(other)),
        out_specs=[whole] * RING,
        out_shape=[jax.ShapeDtypeStruct((pairs, 2, BW, BW), jnp.bfloat16)] * RING,
        scratch_shapes=[
            pltpu.VMEM((2 * BW, K * 2 * BW), jnp.bfloat16),
            pltpu.VMEM((reach * BW, K * 2 * BW), jnp.bfloat16),
            pltpu.VMEM((reach * BW, K * 2 * BW), jnp.bfloat16),
        ],
        compiler_params=pltpu.CompilerParams(vmem_limit_bytes=VMEM_LIMIT),
        cost_estimate=pl.CostEstimate(flops=1, bytes_accessed=1, transcendentals=0),
    )(*mine, *other)


PLANE = {0: (0, 1, 2), 1: (0, 1, 2), 2: (0, 1, 2), 3: (0,)}
NEAR = {0: (3, 4), 1: (3, 4), 2: (3, 4), 3: (1, 2)}
FAR = {3: (3, 4)}


def slots_kernel(offsets, counts, *refs):
    out = refs[-1]
    y, count = lax.axis_index("y"), counts[0]
    parts = [refs[at * RING : (at + 1) * RING] for at in range(3)]

    def place(target):
        for group, wanted in zip(parts, (PLANE, NEAR, FAR)):
            for at, offset in enumerate(wanted.get(target, ())):
                slot = 0
                for step in range(1, SLOTS):
                    slot += jnp.where(offsets[0, step] == offset, step, 0)
                live = (slot < count).astype(jnp.float32)
                for distance in range(RING):
                    band = (target - distance) % RING
                    out[slot, :, band] = group[distance][at].astype(jnp.float32) * live

    for target in range(RING):
        pl.when(y == target)(functools.partial(place, target))


def slots_output(offsets, counts, parts):
    whole = pl.BlockSpec(memory_space=pltpu.VMEM)
    return pl.pallas_call(
        slots_kernel,
        in_specs=[pl.BlockSpec(memory_space=pltpu.SMEM)] * 2 + [whole] * (3 * RING),
        out_specs=whole,
        out_shape=jax.ShapeDtypeStruct((SLOTS, 2, RING, BW, BW), jnp.float32),
        compiler_params=pltpu.CompilerParams(vmem_limit_bytes=VMEM_LIMIT),
    )(offsets, counts, *parts)


def sent_to(targets, pieces):
    moved = [pieces[0]]
    for distance in range(1, RING):
        routes = [((target - distance) % RING, target) for target in targets]
        moved.append(lax.ppermute(pieces[distance], "y", routes))
    return moved


def body(table, series, tapers, live_channels, pair_offset, pair_count):
    swap = [(0, 1), (1, 0)]
    next_plane = [(i, (i - 1) % RING) for i in range(RING)]
    spectra = block_spectra(live_channels, series[0], tapers, table)
    mine = lax.all_to_all(spectra, ("y", "freq"), 0, 0)
    near = lax.ppermute(mine[:RING], "z", next_plane)
    far = lax.ppermute(mine[RING : 2 * RING], "z", next_plane)
    other = lax.ppermute(mine, "core", swap)
    plane = pair_products(PLANE, [mine], [other])
    near, _ = lax.optimization_barrier((near, plane[0]))
    plane = sent_to(PLANE, plane)
    other_near = lax.ppermute(near, "core", swap)
    close = pair_products(NEAR, [mine, near], [other, other_near])
    far, _ = lax.optimization_barrier((far, close[0]))
    close, plane = lax.optimization_barrier((close, plane))
    close = sent_to(NEAR, close)
    other_far = lax.ppermute(far, "core", swap)
    last = pair_products(FAR, [mine, near, far], [other, other_near, other_far])
    last = sent_to(FAR, last)
    parts = plane + close + last
    return slots_output(pair_offset, pair_count, parts)[None]


def solution(mesh):
    table = half_period_tables()
    grid = Mesh(
        mesh.devices.reshape(RING, RING, RING, 2), ("freq", "z", "y", "core")
    )
    blk = ("z", "y", "core")
    return jax.shard_map(
        functools.partial(body, table),
        mesh=grid,
        in_specs=(P(blk, "freq", None), P(), P(blk), P(blk, None), P(blk)),
        out_specs=P(blk, None, None, "freq", None, None),
        check_vma=False,
    )
```

```python
import functools

import jax
import jax.numpy as jnp
import ml_dtypes
import numpy as np
from jax import lax
from jax.experimental import pallas as pl
from jax.experimental.pallas import tpu as pltpu
from jax.sharding import Mesh
from jax.sharding import PartitionSpec as P

NF = 2048
K = 5
BW = 128
PERIOD = 2 * NF
QUARTER = PERIOD // 4
GROUP = BW // 4
SLOTS = 5
RING = 4
OWNERS = RING * RING
WIDTH = 512
VMEM_LIMIT = 24 * 1024 * 1024
STREAM_VMEM_LIMIT = 56 * 1024 * 1024


def quarter_period_tables():
    samples = np.arange(QUARTER, dtype=np.int64)
    owner = np.arange(OWNERS)
    bins = (RING * (owner % RING) + owner // RING)[:, None] * GROUP + np.arange(GROUP)
    angle = (samples[:, None, None] * bins % QUARTER) * (2.0 * np.pi / QUARTER)
    cos, sin = np.cos(angle), np.sin(angle)
    table = np.stack([np.stack([cos, -sin], axis=2), np.stack([sin, cos], axis=2)])
    table = table.reshape(2 * QUARTER, OWNERS * 2 * GROUP).astype(ml_dtypes.bfloat16)
    turn = np.arange(1, 4)[:, None] * samples * (2.0 * np.pi / PERIOD)
    turns = np.stack([np.cos(turn), np.sin(turn)], axis=1).reshape(6, QUARTER)
    return turns.astype(np.float32), table


def spectra_kernel(live_counts, series, tapers, turns, table, out, plain, turned):
    rows, samples = series.shape
    total = K * rows

    @pl.when(pl.program_id(0) == 0)
    def _():
        first = lax.axis_index("freq") * rows
        channel = first + lax.broadcasted_iota(jnp.int32, (rows, QUARTER), 0)
        working = channel < live_counts[0]

        def tapered(k, quarter):
            lanes = slice(quarter * QUARTER, min((quarter + 1) * QUARTER, samples))
            product = series[:, lanes].astype(jnp.float32) * tapers[k : k + 1, lanes]
            short = QUARTER - product.shape[1]
            if short:
                product = jnp.concatenate(
                    [product, jnp.zeros((rows, short), jnp.float32)], axis=1
                )
            product = jnp.where(working, product, 0.0)
            return product.astype(jnp.bfloat16).astype(jnp.float32)

        for k in range(K):
            quarters = [tapered(k, 0) + tapered(k, 4), tapered(k, 1) + tapered(k, 5)]
            quarters += [tapered(k, 2), tapered(k, 3)]
            even, odd = quarters[0] + quarters[2], quarters[1] + quarters[3]
            real, imag = quarters[0] - quarters[2], quarters[1] - quarters[3]
            plain[k * rows : (k + 1) * rows, :] = (even + odd).astype(jnp.bfloat16)
            for r, (p, q) in enumerate(((real, -imag), (even - odd, None), (real, imag))):
                cos, sin = turns[2 * r : 2 * r + 1, :], turns[2 * r + 1 : 2 * r + 2, :]
                at = r * total + k * rows
                left, right = p * cos, -p * sin
                if q is not None:
                    left, right = left + q * sin, right + q * cos
                turned[at : at + rows, :QUARTER] = left.astype(jnp.bfloat16)
                turned[at : at + rows, QUARTER:] = right.astype(jnp.bfloat16)

    groups = [jnp.dot(plain[...], table[:QUARTER, :], preferred_element_type=jnp.float32)]
    others = jnp.dot(turned[...], table[...], preferred_element_type=jnp.float32)
    groups += [others[r * total : (r + 1) * total] for r in range(3)]
    for owner in range(WIDTH // (2 * GROUP)):
        lanes = slice(owner * 2 * GROUP, (owner + 1) * 2 * GROUP)
        for pair in range(2):
            bins = jnp.concatenate([group[:, lanes] for group in groups[2 * pair :][:2]], axis=1)
            out[owner, :, pair * BW : (pair + 1) * BW] = bins.astype(jnp.bfloat16)


def block_spectra(live_counts, series, tapers, turns, table):
    rows, samples = series.shape
    return pl.pallas_call(
        spectra_kernel,
        grid=(OWNERS * 2 * GROUP // WIDTH,),
        in_specs=[
            pl.BlockSpec(memory_space=pltpu.SMEM),
            pl.BlockSpec((rows, samples), lambda step: (0, 0)),
            pl.BlockSpec((K, samples), lambda step: (0, 0)),
            pl.BlockSpec((6, QUARTER), lambda step: (0, 0)),
            pl.BlockSpec((2 * QUARTER, WIDTH), lambda step: (0, step)),
        ],
        out_specs=pl.BlockSpec(
            (WIDTH // (2 * GROUP), K * rows, 2 * BW), lambda step: (step, 0, 0)
        ),
        out_shape=jax.ShapeDtypeStruct((OWNERS, K * rows, 2 * BW), jnp.bfloat16),
        scratch_shapes=[
            pltpu.VMEM((K * rows, QUARTER), jnp.bfloat16),
            pltpu.VMEM((3 * K * rows, 2 * QUARTER), jnp.bfloat16),
        ],
        compiler_params=pltpu.CompilerParams(vmem_limit_bytes=STREAM_VMEM_LIMIT),
    )(live_counts, series, tapers, turns, table)


def pair_kernel(wanted, *refs):
    later, mine_wide, other_wide = refs[-3:]
    outs = refs[-3 - RING : -3]
    inputs = refs[: -3 - RING]
    y, core = lax.axis_index("y"), lax.axis_index("core")
    rows = inputs[0].shape[1] // K
    lane = lax.broadcasted_iota(jnp.int32, (BW, BW), 1)
    is_real = lane % (2 * GROUP) < GROUP
    first = min(wanted)

    def channels(group, at, k):
        for source in group:
            if at < source.shape[0] // RING:
                piece = source[RING * at : RING * (at + 1), k * rows : (k + 1) * rows, :]
                return piece.reshape(RING * rows, 2 * BW)
            at -= source.shape[0] // RING

    def widened(group, wide, blocks):
        for block in blocks:
            to = (block - first) * BW
            for k in range(K):
                wide[to : to + BW, k * 2 * BW : (k + 1) * 2 * BW] = channels(group, block, k)

    same_of, crossed_of = {}, {}
    for target, offsets in wanted.items():
        same_of[target] = [target + offset // 2 for offset in offsets if offset % 2 == 0]
        crossed_of[target] = [target + offset // 2 for offset in offsets if offset % 2 == 1]
    same_blocks = set(wanted).union(*same_of.values())
    crossed_blocks = set().union(*crossed_of.values())
    widened(inputs[: len(inputs) // 2], mine_wide, sorted(same_blocks))
    widened(
        inputs[len(inputs) // 2 :],
        other_wide,
        sorted(crossed_blocks | {block + 1 for block in crossed_blocks}),
    )

    contract = (((1,), (1,)), ((), ()))
    for target, offsets in wanted.items():
        to = (target - first) * BW
        later[:BW, :] = mine_wide[to : to + BW, :]
        for part in range(2 * K):
            at = part * BW
            wide = mine_wide[to : to + BW, at : at + BW].astype(jnp.float32)
            turned = jnp.where(
                is_real, pltpu.roll(wide, BW - GROUP, 1), -pltpu.roll(wide, GROUP, 1)
            )
            later[BW:, at : at + BW] = turned.astype(jnp.bfloat16)
        same, crossed = same_of[target], crossed_of[target]
        at = (same[0] - first) * BW
        partners = mine_wide[at : at + len(same) * BW, :]
        even = lax.dot_general(later[...], partners, contract, preferred_element_type=jnp.float32)
        even = (even * (1.0 / (K * BW))).astype(jnp.bfloat16)
        if crossed:
            at = pl.multiple_of((crossed[0] - first + core) * BW, BW)
            partners = other_wide[pl.ds(at, len(crossed) * BW), :]
            odd = lax.dot_general(
                later[...], partners, contract, preferred_element_type=jnp.float32
            )
            odd = (odd * (1.0 / (K * BW))).astype(jnp.bfloat16)
        distance = lax.rem(target - y + RING, RING)
        for step in range(RING):

            @pl.when(distance == step)
            def _():
                for at, offset in enumerate(offsets):
                    group, kind = (even, same) if offset % 2 == 0 else (odd, crossed)
                    column = kind.index(target + offset // 2) * BW
                    piece = group[:, column : column + BW]
                    outs[step][at, 0] = piece[:BW]
                    outs[step][at, 1] = piece[BW:]


def pair_products(wanted, mine, other):
    pairs = max(len(offsets) for offsets in wanted.values())
    reach = sum(block.shape[0] // RING for block in mine) - min(wanted)
    whole = pl.BlockSpec(memory_space=pltpu.VMEM)
    return pl.pallas_call(
        functools.partial(pair_kernel, wanted),
        in_specs=[whole] * (len(mine) + len(other)),
        out_specs=[whole] * RING,
        out_shape=[jax.ShapeDtypeStruct((pairs, 2, BW, BW), jnp.bfloat16)] * RING,
        scratch_shapes=[
            pltpu.VMEM((2 * BW, K * 2 * BW), jnp.bfloat16),
            pltpu.VMEM((reach * BW, K * 2 * BW), jnp.bfloat16),
            pltpu.VMEM((reach * BW, K * 2 * BW), jnp.bfloat16),
        ],
        compiler_params=pltpu.CompilerParams(vmem_limit_bytes=VMEM_LIMIT),
        cost_estimate=pl.CostEstimate(flops=1, bytes_accessed=1, transcendentals=0),
    )(*mine, *other)


PLANE = {0: (0, 1, 2), 1: (0, 1, 2), 2: (0, 1, 2), 3: (0,)}
NEAR = {0: (3, 4), 1: (3, 4), 2: (3, 4), 3: (1, 2)}
FAR = {3: (3, 4)}


def slots_kernel(offsets, counts, *refs):
    out = refs[-1]
    y, count = lax.axis_index("y"), counts[0]
    parts = [refs[at * RING : (at + 1) * RING] for at in range(3)]

    def place(target):
        for group, wanted in zip(parts, (PLANE, NEAR, FAR)):
            for at, offset in enumerate(wanted.get(target, ())):
                slot = 0
                for step in range(1, SLOTS):
                    slot += jnp.where(offsets[0, step] == offset, step, 0)
                live = (slot < count).astype(jnp.float32)
                for distance in range(RING):
                    band = (target - distance) % RING
                    out[slot, :, band] = group[distance][at].astype(jnp.float32) * live

    for target in range(RING):
        pl.when(y == target)(functools.partial(place, target))


def slots_output(offsets, counts, parts):
    whole = pl.BlockSpec(memory_space=pltpu.VMEM)
    return pl.pallas_call(
        slots_kernel,
        in_specs=[pl.BlockSpec(memory_space=pltpu.SMEM)] * 2 + [whole] * (3 * RING),
        out_specs=whole,
        out_shape=jax.ShapeDtypeStruct((SLOTS, 2, RING, BW, BW), jnp.float32),
        compiler_params=pltpu.CompilerParams(vmem_limit_bytes=VMEM_LIMIT),
    )(offsets, counts, *parts)


def sent_to(targets, pieces):
    moved = [pieces[0]]
    for distance in range(1, RING):
        routes = [((target - distance) % RING, target) for target in targets]
        moved.append(lax.ppermute(pieces[distance], "y", routes))
    return moved


def body(turns, table, series, tapers, live_channels, pair_offset, pair_count):
    swap = [(0, 1), (1, 0)]
    next_plane = [(i, (i - 1) % RING) for i in range(RING)]
    spectra = block_spectra(live_channels, series[0], tapers, turns, table)
    mine = lax.all_to_all(spectra, ("y", "freq"), 0, 0)
    near = lax.ppermute(mine[:RING], "z", next_plane)
    far = lax.ppermute(mine[RING : 2 * RING], "z", next_plane)
    other = lax.ppermute(mine, "core", swap)
    plane = pair_products(PLANE, [mine], [other])
    near, _ = lax.optimization_barrier((near, plane[0]))
    plane = sent_to(PLANE, plane)
    other_near = lax.ppermute(near, "core", swap)
    close = pair_products(NEAR, [mine, near], [other, other_near])
    far, _ = lax.optimization_barrier((far, close[0]))
    close, plane = lax.optimization_barrier((close, plane))
    close = sent_to(NEAR, close)
    other_far = lax.ppermute(far, "core", swap)
    last = pair_products(FAR, [mine, near, far], [other, other_near, other_far])
    last = sent_to(FAR, last)
    parts = plane + close + last
    return slots_output(pair_offset, pair_count, parts)[None]


def solution(mesh):
    turns, table = quarter_period_tables()
    grid = Mesh(
        mesh.devices.reshape(RING, RING, RING, 2), ("freq", "z", "y", "core")
    )
    blk = ("z", "y", "core")
    return jax.shard_map(
        functools.partial(body, turns, table),
        mesh=grid,
        in_specs=(P(blk, "freq", None), P(), P(blk), P(blk, None), P(blk)),
        out_specs=P(blk, None, None, "freq", None, None),
        check_vma=False,
    )
```

```python
import functools

import jax
import jax.numpy as jnp
import ml_dtypes
import numpy as np
from jax import lax
from jax.experimental import pallas as pl
from jax.experimental.pallas import tpu as pltpu
from jax.sharding import Mesh
from jax.sharding import PartitionSpec as P

NF = 2048
K = 5
BW = 128
PERIOD = 2 * NF
QUARTER = PERIOD // 4
GROUP = BW // 4
SLOTS = 5
RING = 4
OWNERS = RING * RING
WIDTH = 512
VMEM_LIMIT = 24 * 1024 * 1024
STREAM_VMEM_LIMIT = 56 * 1024 * 1024


def quarter_period_tables():
    samples = np.arange(QUARTER, dtype=np.int64)
    owner = np.arange(OWNERS)
    bins = (RING * (owner % RING) + owner // RING)[:, None] * GROUP + np.arange(GROUP)
    angle = (samples[:, None, None] * bins % QUARTER) * (2.0 * np.pi / QUARTER)
    cos, sin = np.cos(angle), np.sin(angle)
    table = np.stack([np.stack([cos, -sin], axis=2), np.stack([sin, cos], axis=2)])
    table = table.reshape(2 * QUARTER, OWNERS * 2 * GROUP).astype(ml_dtypes.bfloat16)
    turn = np.arange(1, 4)[:, None] * samples * (2.0 * np.pi / PERIOD)
    turns = np.stack([np.cos(turn), np.sin(turn)], axis=1).reshape(6, QUARTER)
    return turns.astype(np.float32), table


def spectra_kernel(live_counts, series, tapers, turns, table, out, plain, turned):
    rows, samples = series.shape
    total = K * rows

    @pl.when(pl.program_id(0) == 0)
    def _():
        first = lax.axis_index("freq") * rows
        channel = first + lax.broadcasted_iota(jnp.int32, (rows, QUARTER), 0)
        working = channel < live_counts[0]

        def tapered(k, quarter):
            lanes = slice(quarter * QUARTER, min((quarter + 1) * QUARTER, samples))
            product = series[:, lanes].astype(jnp.float32) * tapers[k : k + 1, lanes]
            short = QUARTER - product.shape[1]
            if short:
                product = jnp.concatenate(
                    [product, jnp.zeros((rows, short), jnp.float32)], axis=1
                )
            product = jnp.where(working, product, 0.0)
            return product.astype(jnp.bfloat16).astype(jnp.float32)

        for k in range(K):
            quarters = [tapered(k, 0) + tapered(k, 4), tapered(k, 1) + tapered(k, 5)]
            quarters += [tapered(k, 2), tapered(k, 3)]
            even, odd = quarters[0] + quarters[2], quarters[1] + quarters[3]
            real, imag = quarters[0] - quarters[2], quarters[1] - quarters[3]
            plain[k * rows : (k + 1) * rows, :] = (even + odd).astype(jnp.bfloat16)
            for r, (p, q) in enumerate(((real, -imag), (even - odd, None), (real, imag))):
                cos, sin = turns[2 * r : 2 * r + 1, :], turns[2 * r + 1 : 2 * r + 2, :]
                at = r * total + k * rows
                left, right = p * cos, -p * sin
                if q is not None:
                    left, right = left + q * sin, right + q * cos
                turned[at : at + rows, :QUARTER] = left.astype(jnp.bfloat16)
                turned[at : at + rows, QUARTER:] = right.astype(jnp.bfloat16)

    groups = [jnp.dot(plain[...], table[:QUARTER, :], preferred_element_type=jnp.float32)]
    others = jnp.dot(turned[...], table[...], preferred_element_type=jnp.float32)
    groups += [others[r * total : (r + 1) * total] for r in range(3)]
    for owner in range(WIDTH // (2 * GROUP)):
        lanes = slice(owner * 2 * GROUP, (owner + 1) * 2 * GROUP)
        for pair in range(2):
            bins = jnp.concatenate([group[:, lanes] for group in groups[2 * pair :][:2]], axis=1)
            out[owner, :, pair * BW : (pair + 1) * BW] = bins.astype(jnp.bfloat16)


def block_spectra(live_counts, series, tapers, turns, table):
    rows, samples = series.shape
    return pl.pallas_call(
        spectra_kernel,
        grid=(OWNERS * 2 * GROUP // WIDTH,),
        in_specs=[
            pl.BlockSpec(memory_space=pltpu.SMEM),
            pl.BlockSpec((rows, samples), lambda step: (0, 0)),
            pl.BlockSpec((K, samples), lambda step: (0, 0)),
            pl.BlockSpec((6, QUARTER), lambda step: (0, 0)),
            pl.BlockSpec((2 * QUARTER, WIDTH), lambda step: (0, step)),
        ],
        out_specs=pl.BlockSpec(
            (WIDTH // (2 * GROUP), K * rows, 2 * BW), lambda step: (step, 0, 0)
        ),
        out_shape=jax.ShapeDtypeStruct((OWNERS, K * rows, 2 * BW), jnp.bfloat16),
        scratch_shapes=[
            pltpu.VMEM((K * rows, QUARTER), jnp.bfloat16),
            pltpu.VMEM((3 * K * rows, 2 * QUARTER), jnp.bfloat16),
        ],
        compiler_params=pltpu.CompilerParams(vmem_limit_bytes=STREAM_VMEM_LIMIT),
    )(live_counts, series, tapers, turns, table)


def pair_kernel(wanted, kept, *refs):
    later, mine_wide, other_wide = refs[-3:]
    outs = refs[-3 - RING : -3]
    inputs = refs[: -3 - RING - kept]
    y, core = lax.axis_index("y"), lax.axis_index("core")
    rows = inputs[0].shape[1] // K
    lane = lax.broadcasted_iota(jnp.int32, (BW, BW), 1)
    is_real = lane % (2 * GROUP) < GROUP
    first = min(wanted)

    def channels(group, at, k):
        for source in group:
            if at < source.shape[0] // RING:
                piece = source[RING * at : RING * (at + 1), k * rows : (k + 1) * rows, :]
                return piece.reshape(RING * rows, 2 * BW)
            at -= source.shape[0] // RING

    def widened(group, wide, blocks):
        for block in blocks:
            to = (block - first) * BW
            for k in range(K):
                wide[to : to + BW, k * 2 * BW : (k + 1) * 2 * BW] = channels(group, block, k)

    same_of, crossed_of = {}, {}
    for target, offsets in wanted.items():
        same_of[target] = [target + offset // 2 for offset in offsets if offset % 2 == 0]
        crossed_of[target] = [target + offset // 2 for offset in offsets if offset % 2 == 1]
    same_blocks = set(wanted).union(*same_of.values())
    crossed_blocks = set().union(*crossed_of.values())
    widened(inputs[: len(inputs) // 2], mine_wide, sorted(same_blocks))
    widened(
        inputs[len(inputs) // 2 :],
        other_wide,
        sorted(crossed_blocks | {block + 1 for block in crossed_blocks}),
    )

    contract = (((1,), (1,)), ((), ()))
    for target, offsets in wanted.items():
        to = (target - first) * BW
        later[:BW, :] = mine_wide[to : to + BW, :]
        for part in range(2 * K):
            at = part * BW
            wide = mine_wide[to : to + BW, at : at + BW].astype(jnp.float32)
            turned = jnp.where(
                is_real, pltpu.roll(wide, BW - GROUP, 1), -pltpu.roll(wide, GROUP, 1)
            )
            later[BW:, at : at + BW] = turned.astype(jnp.bfloat16)
        same, crossed = same_of[target], crossed_of[target]
        at = (same[0] - first) * BW
        partners = mine_wide[at : at + len(same) * BW, :]
        even = lax.dot_general(later[...], partners, contract, preferred_element_type=jnp.float32)
        even = (even * (1.0 / (K * BW))).astype(jnp.bfloat16)
        if crossed:
            at = pl.multiple_of((crossed[0] - first + core) * BW, BW)
            partners = other_wide[pl.ds(at, len(crossed) * BW), :]
            odd = lax.dot_general(
                later[...], partners, contract, preferred_element_type=jnp.float32
            )
            odd = (odd * (1.0 / (K * BW))).astype(jnp.bfloat16)
        distance = lax.rem(target - y + RING, RING)
        for step in range(RING):

            @pl.when(distance == step)
            def _():
                for at, offset in enumerate(offsets):
                    group, kind = (even, same) if offset % 2 == 0 else (odd, crossed)
                    column = kind.index(target + offset // 2) * BW
                    piece = group[:, column : column + BW]
                    outs[step][at, 0] = piece[:BW]
                    outs[step][at, 1] = piece[BW:]


def pair_products(wanted, pairs, mine, other, filled=()):
    reach = sum(block.shape[0] // RING for block in mine) - min(wanted)
    whole = pl.BlockSpec(memory_space=pltpu.VMEM)
    inputs = len(mine) + len(other)
    return pl.pallas_call(
        functools.partial(pair_kernel, wanted, len(filled)),
        in_specs=[whole] * (inputs + len(filled)),
        out_specs=[whole] * RING,
        out_shape=[jax.ShapeDtypeStruct((pairs, 2, BW, BW), jnp.bfloat16)] * RING,
        scratch_shapes=[
            pltpu.VMEM((2 * BW, K * 2 * BW), jnp.bfloat16),
            pltpu.VMEM((reach * BW, K * 2 * BW), jnp.bfloat16),
            pltpu.VMEM((reach * BW, K * 2 * BW), jnp.bfloat16),
        ],
        input_output_aliases={inputs + at: at for at in range(len(filled))},
        compiler_params=pltpu.CompilerParams(vmem_limit_bytes=VMEM_LIMIT),
        cost_estimate=pl.CostEstimate(flops=1, bytes_accessed=1, transcendentals=0),
    )(*mine, *other, *filled)


PLANE = {0: (0, 1, 2), 1: (0, 1, 2), 2: (0, 1, 2), 3: (0,)}
REST = {0: (3, 4), 1: (3, 4)}
AHEAD = {2: (3, 4), 3: (1, 2, 3, 4)}


def slots_kernel(offsets, counts, *refs):
    out = refs[-1]
    y, count = lax.axis_index("y"), counts[0]
    parts = [refs[at * RING : (at + 1) * RING] for at in range(2)]

    def place(target):
        for group, wanted in zip(parts, (PLANE, REST | AHEAD)):
            for at, offset in enumerate(wanted.get(target, ())):
                slot = 0
                for step in range(1, SLOTS):
                    slot += jnp.where(offsets[0, step] == offset, step, 0)
                live = (slot < count).astype(jnp.float32)
                for distance in range(RING):
                    band = (target - distance) % RING
                    out[slot, :, band] = group[distance][at].astype(jnp.float32) * live

    for target in range(RING):
        pl.when(y == target)(functools.partial(place, target))


def slots_output(offsets, counts, parts):
    whole = pl.BlockSpec(memory_space=pltpu.VMEM)
    return pl.pallas_call(
        slots_kernel,
        in_specs=[pl.BlockSpec(memory_space=pltpu.SMEM)] * 2 + [whole] * (2 * RING),
        out_specs=whole,
        out_shape=jax.ShapeDtypeStruct((SLOTS, 2, RING, BW, BW), jnp.float32),
        compiler_params=pltpu.CompilerParams(vmem_limit_bytes=VMEM_LIMIT),
    )(offsets, counts, *parts)


def sent_along(pieces):
    moved = [pieces[0]]
    for distance in range(1, RING):
        routes = [(y, (y + distance) % RING) for y in range(RING)]
        moved.append(lax.ppermute(pieces[distance], "y", routes))
    return moved


def body(turns, table, series, tapers, live_channels, pair_offset, pair_count):
    swap = [(0, 1), (1, 0)]
    next_plane = [(i, (i - 1) % RING) for i in range(RING)]
    spectra = block_spectra(live_channels, series[0], tapers, turns, table)
    mine = lax.all_to_all(spectra, ("y", "freq"), 0, 0)
    ahead = lax.ppermute(mine[: 2 * RING], "z", next_plane)
    other = lax.ppermute(mine, "core", swap)
    plane = sent_along(pair_products(PLANE, 3, [mine], [other]))
    rest = pair_products(REST, 4, [mine], [other])
    ahead, *held = lax.optimization_barrier((ahead, *plane, *rest))
    plane, rest = held[:RING], held[RING:]
    other_ahead = lax.ppermute(ahead, "core", swap)
    rest = pair_products(AHEAD, 4, [mine, ahead], [other, other_ahead], rest)
    parts = plane + sent_along(rest)
    return slots_output(pair_offset, pair_count, parts)[None]


def solution(mesh):
    turns, table = quarter_period_tables()
    grid = Mesh(
        mesh.devices.reshape(RING, RING, RING, 2), ("freq", "z", "y", "core")
    )
    blk = ("z", "y", "core")
    return jax.shard_map(
        functools.partial(body, turns, table),
        mesh=grid,
        in_specs=(P(blk, "freq", None), P(), P(blk), P(blk, None), P(blk)),
        out_specs=P(blk, None, None, "freq", None, None),
        check_vma=False,
    )
```

```python
import functools

import jax
import jax.numpy as jnp
import ml_dtypes
import numpy as np
from jax import lax
from jax.experimental import pallas as pl
from jax.experimental.pallas import tpu as pltpu
from jax.sharding import Mesh
from jax.sharding import PartitionSpec as P

NF = 2048
K = 5
BW = 128
PERIOD = 2 * NF
QUARTER = PERIOD // 4
GROUP = BW // 4
SLOTS = 5
RING = 4
OWNERS = RING * RING
WIDTH = 512
VMEM_LIMIT = 24 * 1024 * 1024
STREAM_VMEM_LIMIT = 56 * 1024 * 1024


def quarter_period_tables():
    samples = np.arange(QUARTER, dtype=np.int64)
    owner = np.arange(OWNERS)
    bins = (RING * (owner % RING) + owner // RING)[:, None] * GROUP + np.arange(GROUP)
    angle = (samples[:, None, None] * bins % QUARTER) * (2.0 * np.pi / QUARTER)
    cos, sin = np.cos(angle), np.sin(angle)
    table = np.stack([np.stack([cos, -sin], axis=2), np.stack([sin, cos], axis=2)])
    table = table.reshape(2 * QUARTER, OWNERS * 2 * GROUP).astype(ml_dtypes.bfloat16)
    turn = np.arange(1, 4)[:, None] * samples * (2.0 * np.pi / PERIOD)
    turns = np.stack([np.cos(turn), np.sin(turn)], axis=1).reshape(6, QUARTER)
    return turns.astype(np.float32), table


def spectra_kernel(*refs):
    live_in, series_in, tapers_in, turns_in, table_in, out = refs[:6]
    live, series, tapers, turns, table, spectra, plain, turned, arrived, sent = refs[6:]
    rows, samples = series.shape
    total = K * rows
    owners = WIDTH // (2 * GROUP)
    steps = OWNERS // owners
    small = ((live_in, live), (series_in, series), (tapers_in, tapers), (turns_in, turns))
    loads = [
        pltpu.make_async_copy(source, to, arrived.at[at]) for at, (source, to) in enumerate(small)
    ]
    for step in range(steps):
        columns = pl.ds(step * WIDTH, WIDTH)
        loads.append(
            pltpu.make_async_copy(
                table_in.at[:, columns], table.at[:, columns], arrived.at[len(small) + step]
            )
        )
    for load in loads[: len(small)]:
        load.start()
    for load in loads[: len(small)]:
        load.wait()
    for load in loads[len(small) :]:
        load.start()

    first = lax.axis_index("freq") * rows
    channel = first + lax.broadcasted_iota(jnp.int32, (rows, QUARTER), 0)
    working = channel < live[0]

    def tapered(k, quarter):
        lanes = slice(quarter * QUARTER, min((quarter + 1) * QUARTER, samples))
        product = series[:, lanes].astype(jnp.float32) * tapers[k : k + 1, lanes]
        short = QUARTER - product.shape[1]
        if short:
            product = jnp.concatenate([product, jnp.zeros((rows, short), jnp.float32)], axis=1)
        product = jnp.where(working, product, 0.0)
        return product.astype(jnp.bfloat16).astype(jnp.float32)

    for k in range(K):
        quarters = [tapered(k, 0) + tapered(k, 4), tapered(k, 1) + tapered(k, 5)]
        quarters += [tapered(k, 2), tapered(k, 3)]
        even, odd = quarters[0] + quarters[2], quarters[1] + quarters[3]
        real, imag = quarters[0] - quarters[2], quarters[1] - quarters[3]
        plain[k * rows : (k + 1) * rows, :] = (even + odd).astype(jnp.bfloat16)
        for r, (p, q) in enumerate(((real, -imag), (even - odd, None), (real, imag))):
            cos, sin = turns[2 * r : 2 * r + 1, :], turns[2 * r + 1 : 2 * r + 2, :]
            at = r * total + k * rows
            left, right = p * cos, -p * sin
            if q is not None:
                left, right = left + q * sin, right + q * cos
            turned[at : at + rows, :QUARTER] = left.astype(jnp.bfloat16)
            turned[at : at + rows, QUARTER:] = right.astype(jnp.bfloat16)

    sends = []
    for step in range(steps):
        loads[len(small) + step].wait()
        columns = slice(step * WIDTH, (step + 1) * WIDTH)
        groups = [
            jnp.dot(plain[...], table[:QUARTER, columns], preferred_element_type=jnp.float32)
        ]
        others = jnp.dot(turned[...], table[:, columns], preferred_element_type=jnp.float32)
        groups += [others[r * total : (r + 1) * total] for r in range(3)]
        for owner in range(owners):
            lanes = slice(owner * 2 * GROUP, (owner + 1) * 2 * GROUP)
            for pair in range(2):
                bins = [group[:, lanes] for group in groups[2 * pair :][:2]]
                spectra[step * owners + owner, :, pair * BW : (pair + 1) * BW] = (
                    jnp.concatenate(bins, axis=1).astype(jnp.bfloat16)
                )
        done = pl.ds(step * owners, owners)
        sends.append(pltpu.make_async_copy(spectra.at[done], out.at[done], sent.at[step]))
        sends[-1].start()
    for send in sends:
        send.wait()


def block_spectra(live_counts, series, tapers, turns, table):
    rows = series.shape[0]
    shape = (OWNERS, K * rows, 2 * BW)
    steps = OWNERS * 2 * GROUP // WIDTH
    return pl.pallas_call(
        spectra_kernel,
        in_specs=[pl.BlockSpec(memory_space=pl.ANY)] * 5,
        out_specs=pl.BlockSpec(memory_space=pl.ANY),
        out_shape=jax.ShapeDtypeStruct(shape, jnp.bfloat16),
        scratch_shapes=[
            pltpu.SMEM(live_counts.shape, live_counts.dtype),
            pltpu.VMEM(series.shape, series.dtype),
            pltpu.VMEM(tapers.shape, tapers.dtype),
            pltpu.VMEM(turns.shape, turns.dtype),
            pltpu.VMEM(table.shape, table.dtype),
            pltpu.VMEM(shape, jnp.bfloat16),
            pltpu.VMEM((K * rows, QUARTER), jnp.bfloat16),
            pltpu.VMEM((3 * K * rows, 2 * QUARTER), jnp.bfloat16),
            pltpu.SemaphoreType.DMA((4 + steps,)),
            pltpu.SemaphoreType.DMA((steps,)),
        ],
        compiler_params=pltpu.CompilerParams(vmem_limit_bytes=STREAM_VMEM_LIMIT),
    )(live_counts, series, tapers, turns, table)


def pair_kernel(wanted, kept, *refs):
    later, mine_wide, other_wide = refs[-3:]
    outs = refs[-3 - RING : -3]
    inputs = refs[: -3 - RING - kept]
    y, core = lax.axis_index("y"), lax.axis_index("core")
    rows = inputs[0].shape[1] // K
    lane = lax.broadcasted_iota(jnp.int32, (BW, BW), 1)
    is_real = lane % (2 * GROUP) < GROUP
    first = min(wanted)

    def channels(group, at, k):
        for source in group:
            if at < source.shape[0] // RING:
                piece = source[RING * at : RING * (at + 1), k * rows : (k + 1) * rows, :]
                return piece.reshape(RING * rows, 2 * BW)
            at -= source.shape[0] // RING

    def widened(group, wide, blocks):
        for block in blocks:
            to = (block - first) * BW
            for k in range(K):
                wide[to : to + BW, k * 2 * BW : (k + 1) * 2 * BW] = channels(group, block, k)

    same_of, crossed_of = {}, {}
    for target, offsets in wanted.items():
        same_of[target] = [target + offset // 2 for offset in offsets if offset % 2 == 0]
        crossed_of[target] = [target + offset // 2 for offset in offsets if offset % 2 == 1]
    same_blocks = set(wanted).union(*same_of.values())
    crossed_blocks = set().union(*crossed_of.values())
    widened(inputs[: len(inputs) // 2], mine_wide, sorted(same_blocks))
    widened(
        inputs[len(inputs) // 2 :],
        other_wide,
        sorted(crossed_blocks | {block + 1 for block in crossed_blocks}),
    )

    contract = (((1,), (1,)), ((), ()))
    for target, offsets in wanted.items():
        to = (target - first) * BW
        later[:BW, :] = mine_wide[to : to + BW, :]
        for part in range(2 * K):
            at = part * BW
            wide = mine_wide[to : to + BW, at : at + BW].astype(jnp.float32)
            turned = jnp.where(
                is_real, pltpu.roll(wide, BW - GROUP, 1), -pltpu.roll(wide, GROUP, 1)
            )
            later[BW:, at : at + BW] = turned.astype(jnp.bfloat16)
        same, crossed = same_of[target], crossed_of[target]
        at = (same[0] - first) * BW
        partners = mine_wide[at : at + len(same) * BW, :]
        even = lax.dot_general(later[...], partners, contract, preferred_element_type=jnp.float32)
        even = (even * (1.0 / (K * BW))).astype(jnp.bfloat16)
        if crossed:
            at = pl.multiple_of((crossed[0] - first + core) * BW, BW)
            partners = other_wide[pl.ds(at, len(crossed) * BW), :]
            odd = lax.dot_general(
                later[...], partners, contract, preferred_element_type=jnp.float32
            )
            odd = (odd * (1.0 / (K * BW))).astype(jnp.bfloat16)
        distance = lax.rem(target - y + RING, RING)
        for step in range(RING):

            @pl.when(distance == step)
            def _():
                for at, offset in enumerate(offsets):
                    group, kind = (even, same) if offset % 2 == 0 else (odd, crossed)
                    column = kind.index(target + offset // 2) * BW
                    piece = group[:, column : column + BW]
                    outs[step][at, 0] = piece[:BW]
                    outs[step][at, 1] = piece[BW:]


def pair_products(wanted, pairs, mine, other, filled=()):
    reach = sum(block.shape[0] // RING for block in mine) - min(wanted)
    whole = pl.BlockSpec(memory_space=pltpu.VMEM)
    inputs = len(mine) + len(other)
    return pl.pallas_call(
        functools.partial(pair_kernel, wanted, len(filled)),
        in_specs=[whole] * (inputs + len(filled)),
        out_specs=[whole] * RING,
        out_shape=[jax.ShapeDtypeStruct((pairs, 2, BW, BW), jnp.bfloat16)] * RING,
        scratch_shapes=[
            pltpu.VMEM((2 * BW, K * 2 * BW), jnp.bfloat16),
            pltpu.VMEM((reach * BW, K * 2 * BW), jnp.bfloat16),
            pltpu.VMEM((reach * BW, K * 2 * BW), jnp.bfloat16),
        ],
        input_output_aliases={inputs + at: at for at in range(len(filled))},
        compiler_params=pltpu.CompilerParams(vmem_limit_bytes=VMEM_LIMIT),
        cost_estimate=pl.CostEstimate(flops=1, bytes_accessed=1, transcendentals=0),
    )(*mine, *other, *filled)


PLANE = {0: (0, 1, 2), 1: (0, 1, 2), 2: (0, 1, 2), 3: (0,)}
REST = {0: (3, 4), 1: (3, 4)}
AHEAD = {2: (3, 4), 3: (1, 2, 3, 4)}


def slots_kernel(sources, offsets, counts, *refs):
    out, wide, done = refs[-3:]
    y, count = lax.axis_index("y"), counts[0]

    def place(target):
        copies = []
        for (distance, first_set), group in zip(sources, refs):
            wanted = PLANE if first_set else REST | AHEAD
            band = (target - distance) % RING
            for at, offset in enumerate(wanted[target]):
                slot = 0
                for step in range(1, SLOTS):
                    slot += jnp.where(offsets[0, step] == offset, step, 0)
                live = (slot < count).astype(jnp.float32)
                piece = len(copies)
                wide[piece] = group[at].astype(jnp.float32) * live
                copies.append(
                    pltpu.make_async_copy(wide.at[piece], out.at[slot, :, band], done.at[piece])
                )
                copies[-1].start()
        for copy in copies:
            copy.wait()

    for target in range(RING):
        pl.when(y == target)(functools.partial(place, target))


def slots_output(offsets, counts, sources, groups, begun=None):
    pieces = max(
        sum(len((PLANE if first_set else REST | AHEAD)[target]) for _, first_set in sources)
        for target in range(RING)
    )
    whole = pl.BlockSpec(memory_space=pltpu.VMEM)
    earlier = [] if begun is None else [begun]
    return pl.pallas_call(
        functools.partial(slots_kernel, sources),
        in_specs=[pl.BlockSpec(memory_space=pltpu.SMEM)] * 2
        + [whole] * len(groups)
        + [pl.BlockSpec(memory_space=pl.ANY)] * len(earlier),
        out_specs=pl.BlockSpec(memory_space=pl.ANY),
        out_shape=jax.ShapeDtypeStruct((SLOTS, 2, RING, BW, BW), jnp.float32),
        scratch_shapes=[
            pltpu.VMEM((pieces, 2, BW, BW), jnp.float32),
            pltpu.SemaphoreType.DMA((pieces,)),
        ],
        input_output_aliases={2 + len(groups): 0} if earlier else {},
        compiler_params=pltpu.CompilerParams(vmem_limit_bytes=VMEM_LIMIT),
        cost_estimate=pl.CostEstimate(flops=1, bytes_accessed=1, transcendentals=0),
    )(offsets, counts, *groups, *earlier)


def sent_along(pieces):
    moved = [pieces[0]]
    for distance in range(1, RING):
        routes = [(y, (y + distance) % RING) for y in range(RING)]
        moved.append(lax.ppermute(pieces[distance], "y", routes))
    return moved


def body(turns, table, series, tapers, live_channels, pair_offset, pair_count):
    swap = [(0, 1), (1, 0)]
    next_plane = [(i, (i - 1) % RING) for i in range(RING)]
    spectra = block_spectra(live_channels, series[0], tapers, turns, table)
    mine = lax.all_to_all(spectra, ("y", "freq"), 0, 0)
    ahead = lax.ppermute(mine[: 2 * RING], "z", next_plane)
    other = lax.ppermute(mine, "core", swap)
    plane = sent_along(pair_products(PLANE, 3, [mine], [other]))
    rest = pair_products(REST, 4, [mine], [other])
    ahead, *held = lax.optimization_barrier((ahead, *plane, *rest))
    plane, rest = held[:RING], held[RING:]
    other_ahead = lax.ppermute(ahead, "core", swap)
    rest = pair_products(AHEAD, 4, [mine, ahead], [other, other_ahead], rest)
    rest = sent_along(rest)
    early = [(distance, True) for distance in range(RING)] + [(0, False)]
    late = [(distance, False) for distance in range(1, RING)]
    out = slots_output(pair_offset, pair_count, early, plane + rest[:1])
    return slots_output(pair_offset, pair_count, late, rest[1:], out)[None]


def solution(mesh):
    turns, table = quarter_period_tables()
    grid = Mesh(
        mesh.devices.reshape(RING, RING, RING, 2), ("freq", "z", "y", "core")
    )
    blk = ("z", "y", "core")
    return jax.shard_map(
        functools.partial(body, turns, table),
        mesh=grid,
        in_specs=(P(blk, "freq", None), P(), P(blk), P(blk, None), P(blk)),
        out_specs=P(blk, None, None, "freq", None, None),
        check_vma=False,
    )
```

```python
import functools

import jax
import jax.numpy as jnp
import ml_dtypes
import numpy as np
from jax import lax
from jax.experimental import pallas as pl
from jax.experimental.pallas import tpu as pltpu
from jax.sharding import Mesh
from jax.sharding import PartitionSpec as P

NF = 2048
K = 5
BW = 128
PERIOD = 2 * NF
QUARTER = PERIOD // 4
GROUP = BW // 4
SLOTS = 5
RING = 4
OWNERS = RING * RING
WIDTH = 512
VMEM_LIMIT = 24 * 1024 * 1024
STREAM_VMEM_LIMIT = 56 * 1024 * 1024


def quarter_period_tables():
    samples = np.arange(QUARTER, dtype=np.int64)
    owner = np.arange(OWNERS)
    bins = (RING * (owner % RING) + owner // RING)[:, None] * GROUP + np.arange(GROUP)
    angle = (samples[:, None, None] * bins % QUARTER) * (2.0 * np.pi / QUARTER)
    cos, sin = np.cos(angle), np.sin(angle)
    table = np.stack([np.stack([cos, -sin], axis=2), np.stack([sin, cos], axis=2)])
    table = table.reshape(2 * QUARTER, OWNERS * 2 * GROUP).astype(ml_dtypes.bfloat16)
    turn = np.arange(1, 4)[:, None] * samples * (2.0 * np.pi / PERIOD)
    turns = np.stack([np.cos(turn), np.sin(turn)], axis=1).reshape(6, QUARTER)
    return turns.astype(np.float32), table


def spectra_kernel(*refs):
    live_in, series_in, tapers_in, turns_in, table_in, out = refs[:6]
    live, series, tapers, turns, table, spectra, plain, turned, arrived, sent = refs[6:]
    rows, samples = series.shape
    total = K * rows
    owners = WIDTH // (2 * GROUP)
    steps = OWNERS // owners
    small = ((live_in, live), (series_in, series), (tapers_in, tapers), (turns_in, turns))
    loads = [
        pltpu.make_async_copy(source, to, arrived.at[at]) for at, (source, to) in enumerate(small)
    ]
    for step in range(steps):
        columns = pl.ds(step * WIDTH, WIDTH)
        loads.append(
            pltpu.make_async_copy(
                table_in.at[:, columns], table.at[:, columns], arrived.at[len(small) + step]
            )
        )
    for load in loads[: len(small)]:
        load.start()
    for load in loads[: len(small)]:
        load.wait()
    for load in loads[len(small) :]:
        load.start()

    first = lax.axis_index("freq") * rows
    channel = first + lax.broadcasted_iota(jnp.int32, (rows, QUARTER), 0)
    working = channel < live[0]

    def tapered(k, quarter):
        lanes = slice(quarter * QUARTER, min((quarter + 1) * QUARTER, samples))
        product = series[:, lanes].astype(jnp.float32) * tapers[k : k + 1, lanes]
        short = QUARTER - product.shape[1]
        if short:
            product = jnp.concatenate([product, jnp.zeros((rows, short), jnp.float32)], axis=1)
        product = jnp.where(working, product, 0.0)
        return product.astype(jnp.bfloat16).astype(jnp.float32)

    for k in range(K):
        quarters = [tapered(k, 0) + tapered(k, 4), tapered(k, 1) + tapered(k, 5)]
        quarters += [tapered(k, 2), tapered(k, 3)]
        even, odd = quarters[0] + quarters[2], quarters[1] + quarters[3]
        real, imag = quarters[0] - quarters[2], quarters[1] - quarters[3]
        plain[k * rows : (k + 1) * rows, :] = (even + odd).astype(jnp.bfloat16)
        for r, (p, q) in enumerate(((real, -imag), (even - odd, None), (real, imag))):
            cos, sin = turns[2 * r : 2 * r + 1, :], turns[2 * r + 1 : 2 * r + 2, :]
            at = r * total + k * rows
            left, right = p * cos, -p * sin
            if q is not None:
                left, right = left + q * sin, right + q * cos
            turned[at : at + rows, :QUARTER] = left.astype(jnp.bfloat16)
            turned[at : at + rows, QUARTER:] = right.astype(jnp.bfloat16)

    sends = []
    for step in range(steps):
        loads[len(small) + step].wait()
        columns = slice(step * WIDTH, (step + 1) * WIDTH)
        groups = [
            jnp.dot(plain[...], table[:QUARTER, columns], preferred_element_type=jnp.float32)
        ]
        others = jnp.dot(turned[...], table[:, columns], preferred_element_type=jnp.float32)
        groups += [others[r * total : (r + 1) * total] for r in range(3)]
        for owner in range(owners):
            lanes = slice(owner * 2 * GROUP, (owner + 1) * 2 * GROUP)
            for pair in range(2):
                bins = [group[:, lanes] for group in groups[2 * pair :][:2]]
                spectra[step * owners + owner, :, pair * BW : (pair + 1) * BW] = (
                    jnp.concatenate(bins, axis=1).astype(jnp.bfloat16)
                )
        done = pl.ds(step * owners, owners)
        sends.append(pltpu.make_async_copy(spectra.at[done], out.at[done], sent.at[step]))
        sends[-1].start()
    for send in sends:
        send.wait()


def block_spectra(live_counts, series, tapers, turns, table):
    rows = series.shape[0]
    shape = (OWNERS, K * rows, 2 * BW)
    steps = OWNERS * 2 * GROUP // WIDTH
    return pl.pallas_call(
        spectra_kernel,
        in_specs=[pl.BlockSpec(memory_space=pl.ANY)] * 5,
        out_specs=pl.BlockSpec(memory_space=pl.ANY),
        out_shape=jax.ShapeDtypeStruct(shape, jnp.bfloat16),
        scratch_shapes=[
            pltpu.SMEM(live_counts.shape, live_counts.dtype),
            pltpu.VMEM(series.shape, series.dtype),
            pltpu.VMEM(tapers.shape, tapers.dtype),
            pltpu.VMEM(turns.shape, turns.dtype),
            pltpu.VMEM(table.shape, table.dtype),
            pltpu.VMEM(shape, jnp.bfloat16),
            pltpu.VMEM((K * rows, QUARTER), jnp.bfloat16),
            pltpu.VMEM((3 * K * rows, 2 * QUARTER), jnp.bfloat16),
            pltpu.SemaphoreType.DMA((4 + steps,)),
            pltpu.SemaphoreType.DMA((steps,)),
        ],
        compiler_params=pltpu.CompilerParams(vmem_limit_bytes=STREAM_VMEM_LIMIT),
    )(live_counts, series, tapers, turns, table)


def pair_kernel(wanted, base, kept, split, *refs):
    later, mine_wide, other_wide = refs[-3:]
    outs = refs[-3 - RING : -3]
    inputs = refs[: -3 - RING - kept]
    y, core = lax.axis_index("y"), lax.axis_index("core")
    rows = inputs[0].shape[1] // K
    lane = lax.broadcasted_iota(jnp.int32, (BW, BW), 1)
    is_real = lane % (2 * GROUP) < GROUP
    first = min(wanted)

    def widened(group, wide, blocks):
        senders = [(source, at) for source in group for at in range(source.shape[0])]
        for block in blocks:
            for part, (source, at) in enumerate(senders[RING * block :][:RING]):
                to = (block - first) * BW + part * rows
                for k in range(K):
                    lanes = slice(k * 2 * BW, (k + 1) * 2 * BW)
                    wide[to : to + rows, lanes] = source[at, k * rows : (k + 1) * rows]

    same_of, crossed_of = {}, {}
    for target, offsets in wanted.items():
        same_of[target] = [target + offset // 2 for offset in offsets if offset % 2 == 0]
        crossed_of[target] = [target + offset // 2 for offset in offsets if offset % 2 == 1]
    same_blocks = set(wanted).union(*same_of.values())
    crossed_blocks = set().union(*crossed_of.values())
    widened(inputs[:split], mine_wide, sorted(same_blocks))
    widened(
        inputs[split:],
        other_wide,
        sorted(crossed_blocks | {block + 1 for block in crossed_blocks}),
    )

    contract = (((1,), (1,)), ((), ()))
    for target, offsets in wanted.items():
        to = (target - first) * BW
        later[:BW, :] = mine_wide[to : to + BW, :]
        for part in range(2 * K):
            at = part * BW
            wide = mine_wide[to : to + BW, at : at + BW].astype(jnp.float32)
            turned = jnp.where(
                is_real, pltpu.roll(wide, BW - GROUP, 1), -pltpu.roll(wide, GROUP, 1)
            )
            later[BW:, at : at + BW] = turned.astype(jnp.bfloat16)
        same, crossed = same_of[target], crossed_of[target]
        at = (same[0] - first) * BW
        partners = mine_wide[at : at + len(same) * BW, :]
        even = lax.dot_general(later[...], partners, contract, preferred_element_type=jnp.float32)
        even = (even * (1.0 / (K * BW))).astype(jnp.bfloat16)
        if crossed:
            at = pl.multiple_of((crossed[0] - first + core) * BW, BW)
            partners = other_wide[pl.ds(at, len(crossed) * BW), :]
            odd = lax.dot_general(
                later[...], partners, contract, preferred_element_type=jnp.float32
            )
            odd = (odd * (1.0 / (K * BW))).astype(jnp.bfloat16)
        distance = lax.rem(target - y + RING, RING)
        for step in range(RING):

            @pl.when(distance == step)
            def _():
                for offset in offsets:
                    at = offset - base
                    group, kind = (even, same) if offset % 2 == 0 else (odd, crossed)
                    column = kind.index(target + offset // 2) * BW
                    piece = group[:, column : column + BW]
                    outs[step][at, 0] = piece[:BW]
                    outs[step][at, 1] = piece[BW:]


def pair_products(wanted, base, pairs, mine, other, filled=()):
    reach = sum(block.shape[0] // RING for block in mine) - min(wanted)
    whole = pl.BlockSpec(memory_space=pltpu.VMEM)
    inputs = len(mine) + len(other)
    return pl.pallas_call(
        functools.partial(pair_kernel, wanted, base, len(filled), len(mine)),
        in_specs=[whole] * (inputs + len(filled)),
        out_specs=[whole] * RING,
        out_shape=[jax.ShapeDtypeStruct((pairs, 2, BW, BW), jnp.bfloat16)] * RING,
        scratch_shapes=[
            pltpu.VMEM((2 * BW, K * 2 * BW), jnp.bfloat16),
            pltpu.VMEM((reach * BW, K * 2 * BW), jnp.bfloat16),
            pltpu.VMEM((reach * BW, K * 2 * BW), jnp.bfloat16),
        ],
        input_output_aliases={inputs + at: at for at in range(len(filled))},
        compiler_params=pltpu.CompilerParams(vmem_limit_bytes=VMEM_LIMIT),
        cost_estimate=pl.CostEstimate(flops=1, bytes_accessed=1, transcendentals=0),
    )(*mine, *other, *filled)


FIRST, SECOND = (0, 1, 2), (3, 4)


def slots_kernel(sources, offsets, counts, *refs):
    out, wide, done = refs[-3:]
    y, count = lax.axis_index("y"), counts[0]

    def place(target):
        copies = []
        for (distance, first_set), group in zip(sources, refs):
            band = (target - distance) % RING
            for at, offset in enumerate(FIRST if first_set else SECOND):
                slot = 0
                for step in range(1, SLOTS):
                    slot += jnp.where(offsets[0, step] == offset, step, 0)
                live = (slot < count).astype(jnp.float32)
                piece = len(copies)
                wide[piece] = group[at].astype(jnp.float32) * live
                copies.append(
                    pltpu.make_async_copy(wide.at[piece], out.at[slot, :, band], done.at[piece])
                )
                copies[-1].start()
        for copy in copies:
            copy.wait()

    for target in range(RING):
        pl.when(y == target)(functools.partial(place, target))


def slots_output(offsets, counts, sources, groups, begun=None):
    pieces = sum(len(FIRST if first_set else SECOND) for _, first_set in sources)
    whole = pl.BlockSpec(memory_space=pltpu.VMEM)
    earlier = [] if begun is None else [begun]
    return pl.pallas_call(
        functools.partial(slots_kernel, sources),
        in_specs=[pl.BlockSpec(memory_space=pltpu.SMEM)] * 2
        + [whole] * len(groups)
        + [pl.BlockSpec(memory_space=pl.ANY)] * len(earlier),
        out_specs=pl.BlockSpec(memory_space=pl.ANY),
        out_shape=jax.ShapeDtypeStruct((SLOTS, 2, RING, BW, BW), jnp.float32),
        scratch_shapes=[
            pltpu.VMEM((pieces, 2, BW, BW), jnp.float32),
            pltpu.SemaphoreType.DMA((pieces,)),
        ],
        input_output_aliases={2 + len(groups): 0} if earlier else {},
        compiler_params=pltpu.CompilerParams(vmem_limit_bytes=VMEM_LIMIT),
        cost_estimate=pl.CostEstimate(flops=1, bytes_accessed=1, transcendentals=0),
    )(offsets, counts, *groups, *earlier)


def sent_along(pieces):
    moved = [pieces[0]]
    for distance in range(1, RING):
        routes = [(y, (y + distance) % RING) for y in range(RING)]
        moved.append(lax.ppermute(pieces[distance], "y", routes))
    return moved


def body(turns, table, series, tapers, live_channels, pair_offset, pair_count):
    swap = [(0, 1), (1, 0)]
    next_plane = [(i, (i - 1) % RING) for i in range(RING)]
    spectra = block_spectra(live_channels, series[0], tapers, turns, table)
    mine = lax.all_to_all(spectra, ("y", "freq"), 0, 0)
    near = lax.ppermute(mine[:RING], "z", next_plane)
    far = lax.ppermute(mine[RING : 2 * RING], "z", next_plane)
    crossing = [((z + 1) % RING * 2, z * 2 + 1) for z in range(RING)]
    other_far = lax.ppermute(mine[RING : 2 * RING], ("z", "core"), crossing)
    other = lax.ppermute(mine, "core", swap)
    in_plane = {0: FIRST, 1: FIRST, 2: FIRST, 3: (0,)}
    plane = pair_products(in_plane, 0, 3, [mine], [other])
    near, *plane = lax.optimization_barrier((near, *plane))
    pieces = [near[:1], near[1:2], near[2:]]
    other_near = [lax.ppermute(piece, "core", swap) for piece in pieces]
    plane = pair_products({3: (1, 2)}, 0, 3, [mine, near], [other, *other_near], plane)
    rest = pair_products({0: SECOND, 1: SECOND}, 3, 2, [mine], [other])
    far, other_far, _, *rest = lax.optimization_barrier((far, other_far, plane[0], *rest))
    plane = sent_along(plane)
    mine, other = [mine, near, far], [other, *other_near, other_far]
    rest = sent_along(pair_products({2: SECOND, 3: SECOND}, 3, 2, mine, other, rest))
    early = [(distance, True) for distance in range(RING)] + [(0, False)]
    late = [(distance, False) for distance in range(1, RING)]
    out = slots_output(pair_offset, pair_count, early, plane + rest[:1])
    return slots_output(pair_offset, pair_count, late, rest[1:], out)[None]


def solution(mesh):
    turns, table = quarter_period_tables()
    grid = Mesh(
        mesh.devices.reshape(RING, RING, RING, 2), ("freq", "z", "y", "core")
    )
    blk = ("z", "y", "core")
    return jax.shard_map(
        functools.partial(body, turns, table),
        mesh=grid,
        in_specs=(P(blk, "freq", None), P(), P(blk), P(blk, None), P(blk)),
        out_specs=P(blk, None, None, "freq", None, None),
        check_vma=False,
    )
```

```python
import functools

import jax
import jax.numpy as jnp
import ml_dtypes
import numpy as np
from jax import lax
from jax.experimental import pallas as pl
from jax.experimental.pallas import tpu as pltpu
from jax.sharding import Mesh
from jax.sharding import PartitionSpec as P

NF = 2048
K = 5
BW = 128
PERIOD = 2 * NF
QUARTER = PERIOD // 4
GROUP = BW // 4
SLOTS = 5
RING = 4
OWNERS = RING * RING
WIDTH = 512
VMEM_LIMIT = 24 * 1024 * 1024
STREAM_VMEM_LIMIT = 56 * 1024 * 1024


def quarter_period_tables():
    samples = np.arange(QUARTER, dtype=np.int64)
    owner = np.arange(OWNERS)
    bins = (RING * (owner % RING) + owner // RING)[:, None] * GROUP + np.arange(GROUP)
    angle = (samples[:, None, None] * bins % QUARTER) * (2.0 * np.pi / QUARTER)
    cos, sin = np.cos(angle), np.sin(angle)
    table = np.stack([np.stack([cos, -sin], axis=2), np.stack([sin, cos], axis=2)])
    table = table.reshape(2 * QUARTER, OWNERS * 2 * GROUP).astype(ml_dtypes.bfloat16)
    turn = np.arange(1, 4)[:, None] * samples * (2.0 * np.pi / PERIOD)
    turns = np.stack([np.cos(turn), np.sin(turn)], axis=1).reshape(6, QUARTER)
    return turns.astype(np.float32), table


def spectra_kernel(*refs):
    live_in, series_in, tapers_in, turns_in, table_in, out = refs[:6]
    live, series, tapers, turns, table, spectra, plain, turned, arrived, sent = refs[6:]
    rows, samples = series.shape
    total = K * rows
    owners = WIDTH // (2 * GROUP)
    steps = OWNERS // owners
    small = ((live_in, live), (series_in, series), (tapers_in, tapers), (turns_in, turns))
    loads = [
        pltpu.make_async_copy(source, to, arrived.at[at]) for at, (source, to) in enumerate(small)
    ]
    for step in range(steps):
        columns = pl.ds(step * WIDTH, WIDTH)
        loads.append(
            pltpu.make_async_copy(
                table_in.at[:, columns], table.at[:, columns], arrived.at[len(small) + step]
            )
        )
    for load in loads[: len(small)]:
        load.start()
    for load in loads[: len(small)]:
        load.wait()
    for load in loads[len(small) :]:
        load.start()

    first = lax.axis_index("freq") * rows
    channel = first + lax.broadcasted_iota(jnp.int32, (rows, QUARTER), 0)
    working = channel < live[0]

    def tapered(k, quarter):
        lanes = slice(quarter * QUARTER, min((quarter + 1) * QUARTER, samples))
        product = series[:, lanes].astype(jnp.float32) * tapers[k : k + 1, lanes]
        short = QUARTER - product.shape[1]
        if short:
            product = jnp.concatenate([product, jnp.zeros((rows, short), jnp.float32)], axis=1)
        product = jnp.where(working, product, 0.0)
        return product.astype(jnp.bfloat16).astype(jnp.float32)

    for k in range(K):
        quarters = [tapered(k, 0) + tapered(k, 4), tapered(k, 1) + tapered(k, 5)]
        quarters += [tapered(k, 2), tapered(k, 3)]
        even, odd = quarters[0] + quarters[2], quarters[1] + quarters[3]
        real, imag = quarters[0] - quarters[2], quarters[1] - quarters[3]
        plain[k * rows : (k + 1) * rows, :] = (even + odd).astype(jnp.bfloat16)
        for r, (p, q) in enumerate(((real, -imag), (even - odd, None), (real, imag))):
            cos, sin = turns[2 * r : 2 * r + 1, :], turns[2 * r + 1 : 2 * r + 2, :]
            at = r * total + k * rows
            left, right = p * cos, -p * sin
            if q is not None:
                left, right = left + q * sin, right + q * cos
            turned[at : at + rows, :QUARTER] = left.astype(jnp.bfloat16)
            turned[at : at + rows, QUARTER:] = right.astype(jnp.bfloat16)

    sends = []
    for step in range(steps):
        loads[len(small) + step].wait()
        columns = slice(step * WIDTH, (step + 1) * WIDTH)
        groups = [
            jnp.dot(plain[...], table[:QUARTER, columns], preferred_element_type=jnp.float32)
        ]
        others = jnp.dot(turned[...], table[:, columns], preferred_element_type=jnp.float32)
        groups += [others[r * total : (r + 1) * total] for r in range(3)]
        for owner in range(owners):
            lanes = slice(owner * 2 * GROUP, (owner + 1) * 2 * GROUP)
            for pair in range(2):
                bins = [group[:, lanes] for group in groups[2 * pair :][:2]]
                spectra[step * owners + owner, :, pair * BW : (pair + 1) * BW] = (
                    jnp.concatenate(bins, axis=1).astype(jnp.bfloat16)
                )
        done = pl.ds(step * owners, owners)
        sends.append(pltpu.make_async_copy(spectra.at[done], out.at[done], sent.at[step]))
        sends[-1].start()
    for send in sends:
        send.wait()


def block_spectra(live_counts, series, tapers, turns, table):
    rows = series.shape[0]
    shape = (OWNERS, K * rows, 2 * BW)
    steps = OWNERS * 2 * GROUP // WIDTH
    return pl.pallas_call(
        spectra_kernel,
        in_specs=[pl.BlockSpec(memory_space=pl.ANY)] * 5,
        out_specs=pl.BlockSpec(memory_space=pl.ANY),
        out_shape=jax.ShapeDtypeStruct(shape, jnp.bfloat16),
        scratch_shapes=[
            pltpu.SMEM(live_counts.shape, live_counts.dtype),
            pltpu.VMEM(series.shape, series.dtype),
            pltpu.VMEM(tapers.shape, tapers.dtype),
            pltpu.VMEM(turns.shape, turns.dtype),
            pltpu.VMEM(table.shape, table.dtype),
            pltpu.VMEM(shape, jnp.bfloat16),
            pltpu.VMEM((K * rows, QUARTER), jnp.bfloat16),
            pltpu.VMEM((3 * K * rows, 2 * QUARTER), jnp.bfloat16),
            pltpu.SemaphoreType.DMA((4 + steps,)),
            pltpu.SemaphoreType.DMA((steps,)),
        ],
        compiler_params=pltpu.CompilerParams(vmem_limit_bytes=STREAM_VMEM_LIMIT),
    )(live_counts, series, tapers, turns, table)


def plane_of(offset, base):
    return 2 * (offset - base) - (1 if base == 0 and offset > 0 else 0)


def pair_kernel(wanted, base, kept, split, *refs):
    later, mine_wide, other_wide = refs[-3:]
    outs = refs[-3 - RING : -3]
    inputs = refs[: -3 - RING - kept]
    y, core = lax.axis_index("y"), lax.axis_index("core")
    rows = inputs[0].shape[1] // K
    lane = lax.broadcasted_iota(jnp.int32, (BW, BW), 1)
    is_real = lane % (2 * GROUP) < GROUP
    row = lax.broadcasted_iota(jnp.int32, (BW, BW), 0)
    below, diagonal = row > lane, row == lane
    first = min(wanted)

    def widened(group, wide, blocks):
        senders = [(source, at) for source in group for at in range(source.shape[0])]
        for block in blocks:
            for part, (source, at) in enumerate(senders[RING * block :][:RING]):
                to = (block - first) * BW + part * rows
                for k in range(K):
                    lanes = slice(k * 2 * BW, (k + 1) * 2 * BW)
                    wide[to : to + rows, lanes] = source[at, k * rows : (k + 1) * rows]

    same_of, crossed_of = {}, {}
    for target, offsets in wanted.items():
        same_of[target] = [target + offset // 2 for offset in offsets if offset % 2 == 0]
        crossed_of[target] = [target + offset // 2 for offset in offsets if offset % 2 == 1]
    same_blocks = set(wanted).union(*same_of.values())
    crossed_blocks = set().union(*crossed_of.values())
    widened(inputs[:split], mine_wide, sorted(same_blocks))
    widened(
        inputs[split:],
        other_wide,
        sorted(crossed_blocks | {block + 1 for block in crossed_blocks}),
    )

    contract = (((1,), (1,)), ((), ()))
    for target, offsets in wanted.items():
        to = (target - first) * BW
        later[:BW, :] = mine_wide[to : to + BW, :]
        for part in range(2 * K):
            at = part * BW
            wide = mine_wide[to : to + BW, at : at + BW].astype(jnp.float32)
            turned = jnp.where(
                is_real, pltpu.roll(wide, BW - GROUP, 1), -pltpu.roll(wide, GROUP, 1)
            )
            later[BW:, at : at + BW] = turned.astype(jnp.bfloat16)
        same, crossed = same_of[target], crossed_of[target]
        at = (same[0] - first) * BW
        partners = mine_wide[at : at + len(same) * BW, :]
        even = lax.dot_general(later[...], partners, contract, preferred_element_type=jnp.float32)
        even = (even * (1.0 / (K * BW))).astype(jnp.bfloat16)
        if crossed:
            at = pl.multiple_of((crossed[0] - first + core) * BW, BW)
            partners = other_wide[pl.ds(at, len(crossed) * BW), :]
            odd = lax.dot_general(
                later[...], partners, contract, preferred_element_type=jnp.float32
            )
            odd = (odd * (1.0 / (K * BW))).astype(jnp.bfloat16)
        distance = lax.rem(target - y + RING, RING)
        for step in range(RING):

            @pl.when(distance == step)
            def _():
                for offset in offsets:
                    group, kind = (even, same) if offset % 2 == 0 else (odd, crossed)
                    column = kind.index(target + offset // 2) * BW
                    piece = group[:, column : column + BW]
                    at = plane_of(offset, base)
                    if offset == 0:
                        both = piece.astype(jnp.float32)
                        both = jnp.where(below | diagonal, both[:BW], both[BW:])
                        outs[step][at] = both.astype(jnp.bfloat16)
                    else:
                        outs[step][at] = piece[:BW]
                        outs[step][at + 1] = piece[BW:]


def pair_products(wanted, base, planes, mine, other, filled=()):
    reach = sum(block.shape[0] // RING for block in mine) - min(wanted)
    whole = pl.BlockSpec(memory_space=pltpu.VMEM)
    inputs = len(mine) + len(other)
    return pl.pallas_call(
        functools.partial(pair_kernel, wanted, base, len(filled), len(mine)),
        in_specs=[whole] * (inputs + len(filled)),
        out_specs=[whole] * RING,
        out_shape=[jax.ShapeDtypeStruct((planes, BW, BW), jnp.bfloat16)] * RING,
        scratch_shapes=[
            pltpu.VMEM((2 * BW, K * 2 * BW), jnp.bfloat16),
            pltpu.VMEM((reach * BW, K * 2 * BW), jnp.bfloat16),
            pltpu.VMEM((reach * BW, K * 2 * BW), jnp.bfloat16),
        ],
        input_output_aliases={inputs + at: at for at in range(len(filled))},
        compiler_params=pltpu.CompilerParams(vmem_limit_bytes=VMEM_LIMIT),
        cost_estimate=pl.CostEstimate(flops=1, bytes_accessed=1, transcendentals=0),
    )(*mine, *other, *filled)


FIRST, SECOND = (0, 1, 2), (3, 4)


def slots_kernel(sources, offsets, counts, *refs):
    out, wide, done = refs[-3:]
    y, count = lax.axis_index("y"), counts[0]
    row = lax.broadcasted_iota(jnp.int32, (BW, BW), 0)
    column = lax.broadcasted_iota(jnp.int32, (BW, BW), 1)
    below, diagonal = row > column, row == column

    def place(target):
        copies = []
        for (distance, first_set), group in zip(sources, refs):
            band = (target - distance) % RING
            for offset in FIRST if first_set else SECOND:
                slot = 0
                for step in range(1, SLOTS):
                    slot += jnp.where(offsets[0, step] == offset, step, 0)
                live = (slot < count).astype(jnp.float32)
                piece = len(copies)
                at = plane_of(offset, FIRST[0] if first_set else SECOND[0])
                if offset == 0:
                    both = group[at].astype(jnp.float32)
                    across = both.T
                    wide[piece, 0] = jnp.where(below | diagonal, both, across) * live
                    imag = jnp.where(below, -across, jnp.where(diagonal, 0.0, both))
                    wide[piece, 1] = imag * live
                else:
                    wide[piece] = group[at : at + 2].astype(jnp.float32) * live
                copies.append(
                    pltpu.make_async_copy(wide.at[piece], out.at[slot, :, band], done.at[piece])
                )
                copies[-1].start()
        for copy in copies:
            copy.wait()

    for target in range(RING):
        pl.when(y == target)(functools.partial(place, target))


def slots_output(offsets, counts, sources, groups, begun=None):
    pieces = sum(len(FIRST if first_set else SECOND) for _, first_set in sources)
    whole = pl.BlockSpec(memory_space=pltpu.VMEM)
    earlier = [] if begun is None else [begun]
    return pl.pallas_call(
        functools.partial(slots_kernel, sources),
        in_specs=[pl.BlockSpec(memory_space=pltpu.SMEM)] * 2
        + [whole] * len(groups)
        + [pl.BlockSpec(memory_space=pl.ANY)] * len(earlier),
        out_specs=pl.BlockSpec(memory_space=pl.ANY),
        out_shape=jax.ShapeDtypeStruct((SLOTS, 2, RING, BW, BW), jnp.float32),
        scratch_shapes=[
            pltpu.VMEM((pieces, 2, BW, BW), jnp.float32),
            pltpu.SemaphoreType.DMA((pieces,)),
        ],
        input_output_aliases={2 + len(groups): 0} if earlier else {},
        compiler_params=pltpu.CompilerParams(vmem_limit_bytes=VMEM_LIMIT),
        cost_estimate=pl.CostEstimate(flops=1, bytes_accessed=1, transcendentals=0),
    )(offsets, counts, *groups, *earlier)


def sent_along(pieces):
    moved = [pieces[0]]
    for distance in range(1, RING):
        routes = [(y, (y + distance) % RING) for y in range(RING)]
        moved.append(lax.ppermute(pieces[distance], "y", routes))
    return moved


def body(turns, table, series, tapers, live_channels, pair_offset, pair_count):
    swap = [(0, 1), (1, 0)]
    next_plane = [(i, (i - 1) % RING) for i in range(RING)]
    spectra = block_spectra(live_channels, series[0], tapers, turns, table)
    mine = lax.all_to_all(spectra, ("y", "freq"), 0, 0)
    near = lax.ppermute(mine[:RING], "z", next_plane)
    far = lax.ppermute(mine[RING : 2 * RING], "z", next_plane)
    crossing = [((z + 1) % RING * 2, z * 2 + 1) for z in range(RING)]
    other_far = lax.ppermute(mine[RING : 2 * RING], ("z", "core"), crossing)
    other = lax.ppermute(mine, "core", swap)
    in_plane = {0: FIRST, 1: FIRST, 2: FIRST, 3: (0,)}
    plane = pair_products(in_plane, 0, 5, [mine], [other])
    near, *plane = lax.optimization_barrier((near, *plane))
    pieces = [near[:1], near[1:2], near[2:]]
    other_near = [lax.ppermute(piece, "core", swap) for piece in pieces]
    plane = pair_products({3: (1, 2)}, 0, 5, [mine, near], [other, *other_near], plane)
    close = {0: SECOND, 1: SECOND, 2: SECOND}
    rest = pair_products(close, 3, 4, [mine, near], [other, *other_near])
    far, other_far, _, *rest = lax.optimization_barrier((far, other_far, plane[0], *rest))
    plane = sent_along(plane)
    mine, other = [mine, near, far], [other, *other_near, other_far]
    rest = sent_along(pair_products({3: SECOND}, 3, 4, mine, other, rest))
    early = [(distance, True) for distance in range(RING)] + [(0, False)]
    late = [(distance, False) for distance in range(1, RING)]
    out = slots_output(pair_offset, pair_count, early, plane + rest[:1])
    return slots_output(pair_offset, pair_count, late, rest[1:], out)[None]


def solution(mesh):
    turns, table = quarter_period_tables()
    grid = Mesh(
        mesh.devices.reshape(RING, RING, RING, 2), ("freq", "z", "y", "core")
    )
    blk = ("z", "y", "core")
    return jax.shard_map(
        functools.partial(body, turns, table),
        mesh=grid,
        in_specs=(P(blk, "freq", None), P(), P(blk), P(blk, None), P(blk)),
        out_specs=P(blk, None, None, "freq", None, None),
        check_vma=False,
    )
```
